32 devices in a mesh: parts: 2 (over y), patch: 4 (over z), sub: 2 (over x), rep: 2 (over core).
Axes of the slice: x: 2, y: 2, z: 4, core: 2. Of those that a mesh axis runs over, the one named last changes fastest.
Arguments:
- sky_maps: bfloat16 [4, 8, 16384], P(('parts', 'rep'), None, ('patch', 'sub')), parts along dimension 0, may hold values from -6 to 6
- nb_fine: int32 [8, 16384], P(None, ('patch', 'sub')), may hold values from -128 to 128, as said below
- w_fine: float32 [8, 16384], P(None, ('patch', 'sub')), may hold values from 0.25 to 1
- nb_coarse: int32 [8, 1024], P(None, ('patch', 'sub')), may hold values from -128 to 128, as said below
- w_coarse: float32 [8, 1024], P(None, ('patch', 'sub')), may hold values from 0.25 to 1
- conv_fine: bfloat16 [48, 32], replicated, may hold values from -0.875 to 0.875
- conv_coarse: bfloat16 [192, 128], replicated, may hold values from -0.4375 to 0.4375
- head: bfloat16 [160, 8], replicated, may hold values from -0.5 to 0.5
- cotangent: bfloat16 [4, 8, 16384], P(('parts', 'rep'), None, ('patch', 'sub')), parts along dimension 0, may hold values from -6 to 6
Outputs:
- prediction: bfloat16 [4, 8, 16384], P(('parts', 'rep'), None, ('patch', 'sub')), parts along dimension 0
- grad_fine: float32 [96, 32], P('parts'), parts along dimension 0
- grad_coarse: float32 [384, 128], P('parts'), parts along dimension 0
- grad_head: float32 [320, 8], P('parts'), parts along dimension 0
The draws below stay inside these ranges and needn't reach their ends.
There are 2 independent parts, one for each index of `parts`. The reference program is written for one: setup_inputs(seed, part) draws one part's arguments, and reference() takes and returns one part's arrays. A program takes and returns all parts, laid end to end along the dimension named above; an argument that names none is the same for every part. Nothing has to cross between parts.
Inputs may be any that keep to these rules, and one draw needn't show every extreme that they name: `nb_fine`: offsets in the cyclic nested order of the 16384 fine pixels; some are exactly 128 and some exactly -128. `nb_coarse`: offsets in the cyclic nested order of the 1024 coarse pixels; some are exactly 128 and some exactly -128.
All inputs are finite; a program needn't handle non-finite values.
Results may differ from the reference program's by a relative error of at most 0.012.
Values may be sent and summed in bfloat16 or wider, within the bound.
A program may use at most 64 MiB of HBM per device.

```python
import math
import jax
import jax.numpy as jnp
from jax import lax

CHANNELS = 8
FEAT_FINE = 32
FEAT_COARSE = 128
OUT_CH = 8
ORDER = 6
HALO = 128
BATCH = 2
NPIX = 16384
NCOARSE = 1024


def offset_table(seed_key, pixel_count, reach_size):
    offsets = jax.random.randint(seed_key, (8, pixel_count), -reach_size, reach_size + 1)
    position = jnp.arange(pixel_count, dtype=jnp.int32)
    offsets = offsets.at[7].set(jnp.where(position % 64 == 0, reach_size, offsets[7]))
    offsets = offsets.at[6].set(jnp.where(position % 64 == 1, -reach_size, offsets[6]))
    return offsets.astype(jnp.int32)


def draw_nb_fine(key, part):
    key = jax.random.fold_in(key, 11)
    return offset_table(key, NPIX, HALO)


def draw_nb_coarse(key, part):
    key = jax.random.fold_in(key, 12)
    return offset_table(key, NCOARSE, HALO)


def steps_of(own_key, extent, split, smallest, largest):
    level = 1.0
    for dim, blocks in split:
        steps = jax.random.uniform(jax.random.fold_in(jax.random.fold_in(own_key, 6), dim), (blocks,), jnp.float32, smallest / len(split), largest / len(split))
        level = level * jnp.repeat(jnp.exp(steps), extent[dim] // blocks).reshape((-1,) + (1,) * (len(extent) - 1 - dim))
    return level


def noise(stream_key, dims, width, limit, cuts=(), held_as=jnp.bfloat16):
    values = width * jax.random.normal(stream_key, dims, jnp.float32)
    if cuts:
        values = values * steps_of(stream_key, dims, cuts, -0.22, 0.18)
    return jnp.clip(values, -limit, limit).astype(held_as)


def setup_inputs(seed: int = 0, part: int = 0) -> dict:
    key_list = jax.random.split(jax.random.key(seed), 10)
    part_keys = jax.random.split(jax.random.fold_in(key_list[9], part), 10)
    return {
        "sky_maps": noise(part_keys[0], (BATCH, CHANNELS, NPIX), 1.0, 6.0, ((0, 2), (2, 8))),
        "nb_fine": draw_nb_fine(jax.random.fold_in(key_list[9], 71), part),
        "w_fine": jnp.clip(jnp.exp(math.log(1.0) - 1.3862944 * jax.random.uniform(key_list[2], (8, NPIX), jnp.float32) ** steps_of(key_list[2], (8, NPIX), ((1, 8),), -0.2, 0.2)), 0.25, 1.0),
        "nb_coarse": draw_nb_coarse(jax.random.fold_in(key_list[9], 71), part),
        "w_coarse": jnp.clip(jnp.exp(math.log(1.0) - 1.3862944 * jax.random.uniform(key_list[4], (8, NCOARSE), jnp.float32) ** steps_of(key_list[4], (8, NCOARSE), ((1, 8),), -0.2, 0.2)), 0.25, 1.0),
        "conv_fine": noise(key_list[5], (ORDER * CHANNELS, FEAT_FINE), (ORDER * CHANNELS) ** -0.5, 0.875),
        "conv_coarse": noise(key_list[6], (ORDER * FEAT_FINE, FEAT_COARSE), (ORDER * FEAT_FINE) ** -0.5, 0.4375),
        "head": noise(key_list[7], (FEAT_FINE + FEAT_COARSE, OUT_CH), (FEAT_FINE + FEAT_COARSE) ** -0.5, 0.5),
        "cotangent": noise(part_keys[8], (BATCH, OUT_CH, NPIX), 1.0, 6.0, ((0, 2), (2, 8))),
    }


def relax(values, nearby, degree):
    return (degree * values - nearby) * 0.125 - values

def laplace(values, offset, weight):
    count = values.shape[1]
    neighbour = (jnp.arange(count, dtype=jnp.int32)[None, :] + offset + count) % count
    nearby = lax.optimization_barrier(jnp.sum(weight[None, :, :] * values[:, neighbour], axis=1))
    return relax(values, nearby, lax.optimization_barrier(jnp.sum(weight, axis=0)))

def chebyshev(values, offset, weight):
    polys = [values, laplace(values, offset, weight)]
    for level in range(2, ORDER):
        polys.append(2.0 * laplace(polys[-1], offset, weight) - polys[-2])
    return jnp.stack(polys)

def slope(pre_act):
    sigmoid_value = jax.nn.sigmoid(pre_act)
    return sigmoid_value * (1.0 + pre_act * (1.0 - sigmoid_value))

def reference(sky_maps, nb_fine, w_fine, nb_coarse, w_coarse, conv_fine, conv_coarse, head, cotangent):
    loss_scale = 1.0 / math.sqrt(BATCH * NPIX)
    head_fine = head[:FEAT_FINE]
    head_coarse = head[FEAT_FINE:]
    highest = lax.Precision.HIGHEST
    outputs = []
    grad_one = jnp.zeros((ORDER * CHANNELS, FEAT_FINE), jnp.float32)
    grad_two = jnp.zeros((ORDER * FEAT_FINE, FEAT_COARSE), jnp.float32)
    grad_top = jnp.zeros((FEAT_FINE, OUT_CH), jnp.float32)
    grad_low = jnp.zeros((FEAT_COARSE, OUT_CH), jnp.float32)
    for map_index in range(BATCH):
        sky_map = sky_maps[map_index].astype(jnp.float32)
        fine_stack = chebyshev(sky_map, nb_fine, w_fine).reshape(ORDER * CHANNELS, NPIX).astype(jnp.bfloat16)
        fine_pre = jnp.dot(conv_fine.T, fine_stack, preferred_element_type=jnp.float32)
        fine_hidden = jax.nn.silu(fine_pre).astype(jnp.bfloat16)
        pooled = lax.optimization_barrier(jnp.sum(fine_hidden.astype(jnp.float32).reshape(FEAT_FINE, NCOARSE, 16), axis=2)) * 0.0625

        def coarse_poly(field):
            return chebyshev(field, nb_coarse, w_coarse)
        coarse_terms, pullback = jax.vjp(coarse_poly, pooled)
        coarse_stack = coarse_terms.reshape(ORDER * FEAT_FINE, NCOARSE).astype(jnp.bfloat16)
        coarse_pre = jnp.dot(conv_coarse.T, coarse_stack, preferred_element_type=jnp.float32)
        coarse_hidden = jax.nn.silu(coarse_pre).astype(jnp.bfloat16)
        upward = jnp.dot(head_coarse.T, coarse_hidden, preferred_element_type=jnp.float32)
        result = jnp.dot(head_fine.T, fine_hidden, preferred_element_type=jnp.float32) + jnp.repeat(upward, 16, axis=1)
        outputs.append(result.astype(jnp.bfloat16))
        signal = (cotangent[map_index].astype(jnp.float32) * loss_scale).astype(jnp.bfloat16)
        pooled_signal = lax.optimization_barrier(jnp.sum(signal.astype(jnp.float32).reshape(OUT_CH, NCOARSE, 16), axis=2))
        grad_top = grad_top + jnp.dot(fine_hidden, signal.T, preferred_element_type=jnp.float32)
        grad_low = grad_low + jnp.dot(coarse_hidden.astype(jnp.float32), pooled_signal.T, precision=highest)
        coarse_back = jnp.dot(head_coarse.astype(jnp.float32), pooled_signal, precision=highest)
        coarse_delta = (coarse_back * slope(coarse_pre)).astype(jnp.bfloat16)
        grad_two = grad_two + jnp.dot(coarse_stack, coarse_delta.T, preferred_element_type=jnp.float32)
        coarse_adj = jnp.dot(conv_coarse, coarse_delta, preferred_element_type=jnp.float32)
        pooled_grad = pullback(coarse_adj.reshape(ORDER, FEAT_FINE, NCOARSE))[0]
        fine_back = jnp.dot(head_fine, signal, preferred_element_type=jnp.float32) + jnp.repeat(pooled_grad * 0.0625, 16, axis=1)
        fine_delta = (fine_back * slope(fine_pre)).astype(jnp.bfloat16)
        grad_one = grad_one + jnp.dot(fine_stack, fine_delta.T, preferred_element_type=jnp.float32)
    prediction = jnp.stack(outputs)
    return (prediction, grad_one, grad_two, jnp.concatenate([grad_top, grad_low], axis=0))
```

```python
from functools import partial
import math

import jax
import jax.numpy as jnp
from jax import lax
from jax.experimental import pallas as pl
from jax.experimental.pallas import tpu as pltpu
from jax.sharding import PartitionSpec as P

ORDER = 6
LANES = 128
REACH = ORDER - 1
MESH = pl.DeviceIdType.MESH
F32 = jnp.float32
BF16 = jnp.bfloat16


def dot(a, b, dims=((1,), (0,))):
    return lax.dot_general(a, b, (dims, ((), ())), preferred_element_type=F32)


def split2(x):
    high = x.astype(BF16)
    low = (x - high.astype(F32)).astype(BF16)
    return high, low


def gate(v):
    return 0.5 * jnp.tanh(0.5 * v) + 0.5


def window_of(count):
    full = count <= 4 * REACH + 2
    held = count if full else 4 * REACH + 2
    offsets = [d if d <= held // 2 else d - held for d in range(held)]
    peers = [p for p in range(1, held) if full or abs(offsets[p]) <= 2 * REACH]
    return full, held, offsets, peers


def kernel(
    ring, reps, scale, sky, nbf, wf, nbc, wc, conv_f, conv_c, head, cot,
    pred, out_fine, out_coarse, out_head,
    field, nb, wt, idx8, w8, deg, stack, pool, cg, pg, mat, gc, gc_in, pack, pack_in, total, all_in,
    halo_send, halo_recv, cg_send, cg_recv, pg_send, pg_recv, rep_send, rep_recv, all_send, all_recv,
):
    patches, subs = ring
    count = patches * subs
    full, held, offsets, peers = window_of(count)
    me = lax.axis_index("patch") * subs + lax.axis_index("sub")
    rep = lax.axis_index("rep")
    blocks = sky.shape[2] // LANES
    first, last = REACH, REACH + blocks

    def at(d):
        q = lax.rem(me + (d % count), count)
        return {"patch": lax.div(q, subs), "sub": lax.rem(q, subs)}

    partner = {"rep": lax.rem(rep + 1, reps)}
    barrier = pltpu.get_barrier_semaphore()
    for p in peers:
        pl.semaphore_signal(barrier, inc=1, device_id=at(offsets[p]), device_id_type=MESH)
    if full:
        pl.semaphore_signal(barrier, inc=1, device_id=partner, device_id_type=MESH)

    for b in range(blocks):
        rows = slice((first + b) * 8, (first + b + 1) * 8)
        lanes = slice(b * LANES, (b + 1) * LANES)
        field[0, rows, :] = sky[0, :, lanes].astype(F32)
        nb[rows, :] = nbf[:, lanes]
        wt[rows, :] = wf[:, lanes] * 0.125

    pl.semaphore_wait(barrier, len(peers) + (1 if full else 0))

    def push(src, dst, ssem, rsem, to):
        copy = pltpu.make_async_remote_copy(
            src_ref=src, dst_ref=dst, send_sem=ssem, recv_sem=rsem, device_id=to, device_id_type=MESH
        )
        copy.start()
        return copy

    halos = []
    for n, (ref, width) in enumerate(((field.at[0], REACH), (nb, REACH - 1), (wt, REACH - 1))):
        size = width * 8
        skip = (REACH - width) * 8
        halos.append(push(
            ref.at[pl.ds(last * 8 - size, size)], ref.at[pl.ds(skip, size)],
            halo_send.at[2 * n], halo_recv.at[2 * n], at(1)))
        halos.append(push(
            ref.at[pl.ds(first * 8, size)], ref.at[pl.ds(last * 8, size)],
            halo_send.at[2 * n + 1], halo_recv.at[2 * n + 1], at(-1)))

    pixel = lax.broadcasted_iota(jnp.int32, pool.shape, 0)
    coarse = lax.broadcasted_iota(jnp.int32, pool.shape, 1)
    pool[...] = jnp.where((pixel >> 4) == coarse, 1.0, 0.0).astype(BF16)
    signal = (cot[0].astype(F32) * scale).astype(BF16)
    pooled_signal = dot(signal, pool[...])
    cg[0, 0:8, :] = nbc[...].astype(F32)
    cg[0, 8:16, :] = wc[...] * 0.125
    cg[0, 16:24, :] = pooled_signal
    gathers = []
    for p in peers:
        back = (held - p) % held
        gathers.append(push(cg.at[0], cg.at[back], cg_send.at[p], cg_recv.at[back], at(offsets[p])))

    def spread_slots(b0, b1):
        shape = (b1 - b0, 8, LANES)
        rows = slice(b0 * 8, b1 * 8)
        lane = lax.broadcasted_iota(jnp.int32, ((b1 - b0) * 8, LANES), 1)
        near_nb = nb[rows, :].reshape(shape)
        near_w = wt[rows, :].reshape(shape)
        acc = None
        for j in range(8):
            offs = jnp.broadcast_to(near_nb[:, j : j + 1, :], shape).reshape((b1 - b0) * 8, LANES)
            wide = jnp.broadcast_to(near_w[:, j : j + 1, :], shape).reshape((b1 - b0) * 8, LANES)
            idx8[j, rows, :] = offs + lane
            w8[j, rows, :] = wide
            acc = wide if acc is None else acc + wide
        deg[rows, :] = acc - 1.0

    def level(k, b0, b1):
        rows = slice(b0 * 8, b1 * 8)
        lo = field[k - 1, slice(b0 * 8 - 8, b1 * 8 - 8), :]
        mid = field[k - 1, rows, :]
        hi = field[k - 1, slice(b0 * 8 + 8, b1 * 8 + 8), :]
        near = None
        for j in range(8):
            index = idx8[j, rows, :]
            source = index & (LANES - 1)
            g = jnp.where(
                index < 0,
                jnp.take_along_axis(lo, source, axis=1, mode="promise_in_bounds"),
                jnp.where(
                    index >= LANES,
                    jnp.take_along_axis(hi, source, axis=1, mode="promise_in_bounds"),
                    jnp.take_along_axis(mid, source, axis=1, mode="promise_in_bounds"),
                ),
            )
            term = w8[j, rows, :] * g
            near = term if near is None else near + term
        lap = deg[rows, :] * mid - near
        field[k, rows, :] = lap if k == 1 else 2.0 * lap - field[k - 2, rows, :]

    spread_slots(first, last)
    for k in range(1, ORDER):
        level(k, first + k, last - k)
    for copy in halos:
        copy.wait()
    spread_slots(1, first)
    spread_slots(last, last + REACH - 1)
    for k in range(1, ORDER):
        level(k, k, first + k)
        level(k, last - k, last + REACH - k)
    for b in range(blocks):
        tile = field[:, slice((first + b) * 8, (first + b + 1) * 8), :]
        stack[:, slice(b * LANES, (b + 1) * LANES)] = tile.reshape(ORDER * 8, LANES).astype(BF16)

    fine_pre = dot(conv_f[...], stack[...], ((0,), (0,)))
    fine_gate = gate(fine_pre)
    hidden = (fine_pre * fine_gate).astype(BF16)
    pg[0] = dot(hidden, pool[...]) * 0.0625
    pooled_gathers = []
    for p in peers:
        back = (held - p) % held
        pooled_gathers.append(
            push(pg.at[0], pg.at[back], pg_send.at[p], pg_recv.at[back], at(offsets[p])))

    grad_top = dot(signal, hidden, ((1,), (1,)))
    fine_slope = fine_gate * (1.0 + fine_pre * (1.0 - fine_gate))
    head_fine = head[0:32, :]
    head_coarse = head[32:160, :]
    direct = dot(head_fine, signal)
    result_fine = dot(head_fine, hidden, ((0,), (0,)))

    for copy in gathers:
        copy.wait()
    if not full:
        cg[held // 2] = cg[0]
    source = lax.broadcasted_iota(jnp.int32, (3 * LANES, LANES), 0)
    lane = lax.broadcasted_iota(jnp.int32, (8, LANES), 1)
    degrees = []
    for t in range(held):
        offs = cg[t, 0:8, :].astype(jnp.int32) + lane + LANES
        weight = cg[t, 8:16, :]
        block = None
        for j in range(8):
            term = jnp.where(offs[j : j + 1, :] == source, weight[j : j + 1, :], 0.0)
            block = term if block is None else block + term
        u, side = t // 2, t % 2
        cols = slice(side * LANES, (side + 1) * LANES)
        mat[u, slice(side * LANES, (side + 3) * LANES), cols] = block.astype(BF16)
        empty = 3 * LANES if side == 0 else 0
        mat[u, slice(empty, empty + LANES), cols] = jnp.zeros((LANES, LANES), BF16)
        degrees.append(jnp.sum(weight, axis=0, keepdims=True) - 1.0)
    degree = jnp.concatenate(degrees, axis=1)
    signals = jnp.concatenate([cg[t, 16:24, :] for t in range(held)], axis=1)
    sig_high, sig_low = split2(signals)
    coarse_back = dot(head_coarse, sig_high) + dot(head_coarse, sig_low)

    for copy in pooled_gathers:
        copy.wait()
    if not full:
        pg[held // 2] = pg[0]

    wide = held * LANES

    def forward(x):
        rows = x.shape[0]
        high, low = split2(x)
        both = jnp.concatenate([high, low], axis=0)
        both = jnp.concatenate([both[:, wide - LANES :], both, both[:, :LANES]], axis=1)
        parts = []
        for u in range(held // 2):
            got = dot(both[:, 2 * u * LANES : (2 * u + 4) * LANES], mat[u])
            parts.append(got[:rows] + got[rows:])
        return degree * x - jnp.concatenate(parts, axis=1)

    def adjoint(x):
        rows = x.shape[0]
        high, low = split2(x)
        both = jnp.concatenate([high, low], axis=0)
        sums = [None] * held
        for u in range(held // 2):
            got = dot(both[:, 2 * u * LANES : (2 * u + 2) * LANES], mat[u], ((1,), (1,)))
            got = got[:rows] + got[rows:]
            for i in range(4):
                s = (2 * u - 1 + i) % held
                piece = got[:, i * LANES : (i + 1) * LANES]
                sums[s] = piece if sums[s] is None else sums[s] + piece
        return degree * x - jnp.concatenate(sums, axis=1)

    poly = [jnp.concatenate([pg[t] for t in range(held)], axis=1)]
    poly.append(forward(poly[0]))
    for k in range(2, ORDER):
        poly.append(2.0 * forward(poly[-1]) - poly[-2])
    coarse_stack = jnp.concatenate(poly, axis=0).astype(BF16)
    coarse_pre = dot(conv_c[...], coarse_stack, ((0,), (0,)))
    coarse_gate = gate(coarse_pre)
    coarse_hidden = (coarse_pre * coarse_gate).astype(BF16)
    coarse_delta = (
        coarse_back * (coarse_gate * (1.0 + coarse_pre * (1.0 - coarse_gate)))
    ).astype(BF16)
    coarse_adj = dot(conv_c[...], coarse_delta)
    adj = [coarse_adj[32 * k : 32 * (k + 1)] for k in range(ORDER)]
    for k in range(ORDER - 1, 1, -1):
        adj[k - 1] = adj[k - 1] + 2.0 * adjoint(adj[k])
        adj[k - 2] = adj[k - 2] - adj[k]
    pooled_grad = (adj[0] + adjoint(adj[1]))[:, :LANES] * 0.0625

    pool_t = ((1,), (1,))
    grad_high, grad_low_part = split2(pooled_grad)
    raised = dot(jnp.concatenate([grad_high, grad_low_part], axis=0), pool[...], pool_t)
    fine_delta = ((direct + raised[:32] + raised[32:]) * fine_slope).astype(BF16)
    grad_fine = dot(stack[...], fine_delta, pool_t)

    pack[:, 0:32] = grad_fine[0:16]
    pack[:, 32:64] = grad_fine[16:32]
    pack[:, 64:96] = grad_fine[32:48]
    pack[0:8, 96:128] = grad_top
    pack[8:16, 96:128] = jnp.zeros((8, 32), F32)
    if full:
        pair = push(pack, pack_in, rep_send.at[0], rep_recv.at[0], partner)

    span = slice(0, wide if full else LANES)
    gc[0:192, :] = dot(coarse_stack[:, span], coarse_delta[:, span], pool_t)
    gc[192:200, :] = dot(sig_high[:, span], coarse_hidden[:, span], pool_t) + dot(
        sig_low[:, span], coarse_hidden[:, span], pool_t)

    if full:
        pair.wait()
        total[0] = pack[...] + pack_in[...]
        spreads = []
        for p in peers:
            back = (held - p) % held
            spreads.append(
                push(total.at[0], total.at[back], all_send.at[p], all_recv.at[back], at(offsets[p])))
        pair_coarse = push(gc, gc_in, rep_send.at[1], rep_recv.at[1], partner)

    upward = dot(head_coarse, coarse_hidden[:, :LANES], ((0,), (0,)))
    up_high, up_low = split2(upward)
    result = result_fine + dot(up_high, pool[...], pool_t) + dot(up_low, pool[...], pool_t)
    pred[0] = result.astype(BF16)

    if full:
        pair_coarse.wait()
        sums = gc[...] + gc_in[...]
        for copy in spreads:
            copy.wait()
        whole = total[0]
        for t in range(1, held):
            whole = whole + total[t]
    else:
        sums = gc[...]
        whole = pack[...]
    out_coarse[...] = sums[0:192]
    out_fine[0:16, :] = whole[:, 0:32]
    out_fine[16:32, :] = whole[:, 32:64]
    out_fine[32:48, :] = whole[:, 64:96]
    out_head[0:32, :] = jnp.transpose(whole[0:8, 96:128])
    out_head[32:160, :] = jnp.transpose(sums[192:200])


def on_device(ring, reps, *args):
    sky, conv_f, conv_c, head = args[0], args[5], args[6], args[7]
    pixels = sky.shape[2]
    count = ring[0] * ring[1]
    full, held, _, _ = window_of(count)
    rows = (pixels // LANES + 2 * REACH) * 8
    scale = 1.0 / math.sqrt(pixels * count * sky.shape[0] * reps)
    dma = pltpu.SemaphoreType.DMA
    vmem = pl.BlockSpec(memory_space=pltpu.VMEM)
    result = pl.pallas_call(
        partial(kernel, ring, reps, scale),
        out_shape=(
            jax.ShapeDtypeStruct(sky.shape, BF16),
            jax.ShapeDtypeStruct(conv_f.shape, F32),
            jax.ShapeDtypeStruct(conv_c.shape, F32),
            jax.ShapeDtypeStruct(head.shape, F32),
        ),
        in_specs=[vmem] * 9,
        out_specs=(vmem,) * 4,
        scratch_shapes=[
            pltpu.VMEM((ORDER, rows, LANES), F32),
            pltpu.VMEM((rows, LANES), jnp.int32),
            pltpu.VMEM((rows, LANES), F32),
            pltpu.VMEM((8, rows, LANES), jnp.int32),
            pltpu.VMEM((8, rows, LANES), F32),
            pltpu.VMEM((rows, LANES), F32),
            pltpu.VMEM((ORDER * 8, pixels), BF16),
            pltpu.VMEM((pixels, pixels // 16), BF16),
            pltpu.VMEM((held, 24, LANES), F32),
            pltpu.VMEM((held, 32, LANES), F32),
            pltpu.VMEM((held // 2, 4 * LANES, 2 * LANES), BF16),
            pltpu.VMEM((200, LANES), F32),
            pltpu.VMEM((200, LANES), F32),
            pltpu.VMEM((16, LANES), F32),
            pltpu.VMEM((16, LANES), F32),
            pltpu.VMEM((held, 16, LANES), F32),
            pltpu.VMEM((8, LANES), F32),
            dma((6,)), dma((6,)),
            dma((held,)), dma((held,)),
            dma((held,)), dma((held,)),
            dma((2,)), dma((2,)),
            dma((held,)), dma((held,)),
        ],
        compiler_params=pltpu.CompilerParams(
            collective_id=0, has_side_effects=True, vmem_limit_bytes=40 * 1024 * 1024
        ),
        name="unet",
    )(*args)
    if not full:
        pred, grad_fine, grad_coarse, grad_head = result
        grads = lax.psum((grad_fine, grad_coarse, grad_head), ("patch", "sub", "rep"))
        result = (pred, *grads)
    return tuple(result)


def solution(mesh):
    pixel = P(None, ("patch", "sub"))
    maps = P(("parts", "rep"), None, ("patch", "sub"))
    ring = (mesh.shape["patch"], mesh.shape["sub"])
    return jax.shard_map(
        partial(on_device, ring, mesh.shape["rep"]),
        mesh=mesh,
        in_specs=(maps, pixel, pixel, pixel, pixel, P(), P(), P(), maps),
        out_specs=(maps, P("parts", None), P("parts", None), P("parts", None)),
        check_vma=False,
    )
```

```python
from functools import partial
import math

import jax
import jax.numpy as jnp
from jax import lax
from jax.experimental import pallas as pl
from jax.experimental.pallas import tpu as pltpu
from jax.sharding import PartitionSpec as P

ORDER = 6
LANES = 128
REACH = ORDER - 1
VMEM_BYTES = 64 * 1024 * 1024
MESH = pl.DeviceIdType.MESH
F32 = jnp.float32
BF16 = jnp.bfloat16


def dot(a, b, dims=((1,), (0,))):
    return lax.dot_general(a, b, (dims, ((), ())), preferred_element_type=F32)


def split2(x):
    high = x.astype(BF16)
    low = (x - high.astype(F32)).astype(BF16)
    return high, low


def gate(v):
    return 0.5 * jnp.tanh(0.5 * v) + 0.5


def window_of(count):
    full = count <= 4 * REACH + 2
    held = count if full else 4 * REACH + 2
    offsets = [d if d <= held // 2 else d - held for d in range(held)]
    peers = [p for p in range(1, held) if full or abs(offsets[p]) <= 2 * REACH]
    return full, held, offsets, peers


def kernel(
    ring, reps, scale, *refs
):
    hbm = refs[:9]
    results = refs[9:13]
    local = refs[13:22]
    sky, nbf, wf, nbc, wc, conv_f, conv_c, head, cot = local
    (
    field, nb, wt, idx8, w8, deg, stack, pool, cg, pg, mat, gc, gc_in, pack, pack_in, total, all_in,
    halo_send, halo_recv, cg_send, cg_recv, pg_send, pg_recv, rep_send, rep_recv, all_send, all_recv,
        load_sem, pred, out_fine, out_coarse, out_head, store_sem,
    ) = refs[22:]
    loads = [
        pltpu.make_async_copy(hbm[n], local[n], load_sem.at[n]) for n in range(9)
    ]
    for n in (0, 1, 2, 8, 3, 4, 5, 7, 6):
        loads[n].start()
    patches, subs = ring
    count = patches * subs
    full, held, offsets, peers = window_of(count)
    me = lax.axis_index("patch") * subs + lax.axis_index("sub")
    rep = lax.axis_index("rep")
    blocks = sky.shape[2] // LANES
    first, last = REACH, REACH + blocks

    def at(d):
        q = lax.rem(me + (d % count), count)
        return {"patch": lax.div(q, subs), "sub": lax.rem(q, subs)}

    partner = {"rep": lax.rem(rep + 1, reps)}
    barrier = pltpu.get_barrier_semaphore()
    for p in peers:
        pl.semaphore_signal(barrier, inc=1, device_id=at(offsets[p]), device_id_type=MESH)
    if full:
        pl.semaphore_signal(barrier, inc=1, device_id=partner, device_id_type=MESH)

    for n in range(3):
        loads[n].wait()
    for b in range(blocks):
        rows = slice((first + b) * 8, (first + b + 1) * 8)
        lanes = slice(b * LANES, (b + 1) * LANES)
        field[0, rows, :] = sky[0, :, lanes].astype(F32)
        nb[rows, :] = nbf[:, lanes]
        wt[rows, :] = wf[:, lanes] * 0.125

    pl.semaphore_wait(barrier, len(peers) + (1 if full else 0))

    def push(src, dst, ssem, rsem, to):
        copy = pltpu.make_async_remote_copy(
            src_ref=src, dst_ref=dst, send_sem=ssem, recv_sem=rsem, device_id=to, device_id_type=MESH
        )
        copy.start()
        return copy

    halos = []
    for n, (ref, width) in enumerate(((field.at[0], REACH), (nb, REACH - 1), (wt, REACH - 1))):
        size = width * 8
        skip = (REACH - width) * 8
        halos.append(push(
            ref.at[pl.ds(last * 8 - size, size)], ref.at[pl.ds(skip, size)],
            halo_send.at[2 * n], halo_recv.at[2 * n], at(1)))
        halos.append(push(
            ref.at[pl.ds(first * 8, size)], ref.at[pl.ds(last * 8, size)],
            halo_send.at[2 * n + 1], halo_recv.at[2 * n + 1], at(-1)))

    pixel = lax.broadcasted_iota(jnp.int32, pool.shape, 0)
    coarse = lax.broadcasted_iota(jnp.int32, pool.shape, 1)
    pool[...] = jnp.where((pixel >> 4) == coarse, 1.0, 0.0).astype(BF16)
    for n in (8, 3, 4):
        loads[n].wait()
    signal = (cot[0].astype(F32) * scale).astype(BF16)
    pooled_signal = dot(signal, pool[...])
    cg[0, 0:8, :] = nbc[...].astype(F32)
    cg[0, 8:16, :] = wc[...] * 0.125
    cg[0, 16:24, :] = pooled_signal
    gathers = []
    for p in peers:
        back = (held - p) % held
        gathers.append(push(cg.at[0], cg.at[back], cg_send.at[p], cg_recv.at[back], at(offsets[p])))

    def spread_slots(b0, b1):
        shape = (b1 - b0, 8, LANES)
        rows = slice(b0 * 8, b1 * 8)
        lane = lax.broadcasted_iota(jnp.int32, ((b1 - b0) * 8, LANES), 1)
        near_nb = nb[rows, :].reshape(shape)
        near_w = wt[rows, :].reshape(shape)
        acc = None
        for j in range(8):
            offs = jnp.broadcast_to(near_nb[:, j : j + 1, :], shape).reshape((b1 - b0) * 8, LANES)
            wide = jnp.broadcast_to(near_w[:, j : j + 1, :], shape).reshape((b1 - b0) * 8, LANES)
            idx8[j, rows, :] = offs + lane
            w8[j, rows, :] = wide
            acc = wide if acc is None else acc + wide
        deg[rows, :] = acc - 1.0

    def level(k, b0, b1):
        rows = slice(b0 * 8, b1 * 8)
        lo = field[k - 1, slice(b0 * 8 - 8, b1 * 8 - 8), :]
        mid = field[k - 1, rows, :]
        hi = field[k - 1, slice(b0 * 8 + 8, b1 * 8 + 8), :]
        near = None
        for j in range(8):
            index = idx8[j, rows, :]
            source = index & (LANES - 1)
            g = jnp.where(
                index < 0,
                jnp.take_along_axis(lo, source, axis=1, mode="promise_in_bounds"),
                jnp.where(
                    index >= LANES,
                    jnp.take_along_axis(hi, source, axis=1, mode="promise_in_bounds"),
                    jnp.take_along_axis(mid, source, axis=1, mode="promise_in_bounds"),
                ),
            )
            term = w8[j, rows, :] * g
            near = term if near is None else near + term
        lap = deg[rows, :] * mid - near
        field[k, rows, :] = lap if k == 1 else 2.0 * lap - field[k - 2, rows, :]

    spread_slots(first, last)
    for k in range(1, ORDER):
        level(k, first + k, last - k)
    for copy in halos:
        copy.wait()
    spread_slots(1, first)
    spread_slots(last, last + REACH - 1)
    for k in range(1, ORDER):
        level(k, k, first + k)
        level(k, last - k, last + REACH - k)
    for b in range(blocks):
        tile = field[:, slice((first + b) * 8, (first + b + 1) * 8), :]
        stack[:, slice(b * LANES, (b + 1) * LANES)] = tile.reshape(ORDER * 8, LANES).astype(BF16)

    for n in (5, 6, 7):
        loads[n].wait()
    fine_pre = dot(conv_f[...], stack[...])
    fine_gate = gate(fine_pre)
    hidden = (fine_pre * fine_gate).astype(BF16)
    pg[0] = dot(hidden, pool[...]) * 0.0625
    pooled_gathers = []
    for p in peers:
        back = (held - p) % held
        pooled_gathers.append(
            push(pg.at[0], pg.at[back], pg_send.at[p], pg_recv.at[back], at(offsets[p])))

    grad_top = dot(signal, hidden, ((1,), (1,)))
    fine_slope = fine_gate * (1.0 + fine_pre * (1.0 - fine_gate))
    head_fine = head[:, 0:32]
    head_coarse = head[:, 32:160]
    direct = dot(head_fine, signal, ((0,), (0,)))
    result_fine = dot(head_fine, hidden)

    for copy in gathers:
        copy.wait()
    if not full:
        cg[held // 2] = cg[0]
    source = lax.broadcasted_iota(jnp.int32, (3 * LANES, LANES), 0)
    lane = lax.broadcasted_iota(jnp.int32, (8, LANES), 1)
    degrees = []
    for t in range(held):
        offs = cg[t, 0:8, :].astype(jnp.int32) + lane + LANES
        weight = cg[t, 8:16, :]
        block = None
        for j in range(8):
            term = jnp.where(offs[j : j + 1, :] == source, weight[j : j + 1, :], 0.0)
            block = term if block is None else block + term
        u, side = t // 2, t % 2
        cols = slice(side * LANES, (side + 1) * LANES)
        mat[u, slice(side * LANES, (side + 3) * LANES), cols] = block.astype(BF16)
        empty = 3 * LANES if side == 0 else 0
        mat[u, slice(empty, empty + LANES), cols] = jnp.zeros((LANES, LANES), BF16)
        degrees.append(jnp.sum(weight, axis=0, keepdims=True) - 1.0)
    degree = jnp.concatenate(degrees, axis=1)
    signals = jnp.concatenate([cg[t, 16:24, :] for t in range(held)], axis=1)
    sig_high, sig_low = split2(signals)
    coarse_back = dot(head_coarse, sig_high, ((0,), (0,))) + dot(head_coarse, sig_low, ((0,), (0,)))

    for copy in pooled_gathers:
        copy.wait()
    if not full:
        pg[held // 2] = pg[0]

    wide = held * LANES

    def forward(x):
        rows = x.shape[0]
        high, low = split2(x)
        both = jnp.concatenate([high, low], axis=0)
        both = jnp.concatenate([both[:, wide - LANES :], both, both[:, :LANES]], axis=1)
        parts = []
        for u in range(held // 2):
            got = dot(both[:, 2 * u * LANES : (2 * u + 4) * LANES], mat[u])
            parts.append(got[:rows] + got[rows:])
        return degree * x - jnp.concatenate(parts, axis=1)

    def adjoint(x):
        rows = x.shape[0]
        high, low = split2(x)
        both = jnp.concatenate([high, low], axis=0)
        sums = [None] * held
        for u in range(held // 2):
            got = dot(both[:, 2 * u * LANES : (2 * u + 2) * LANES], mat[u], ((1,), (1,)))
            got = got[:rows] + got[rows:]
            for i in range(4):
                s = (2 * u - 1 + i) % held
                piece = got[:, i * LANES : (i + 1) * LANES]
                sums[s] = piece if sums[s] is None else sums[s] + piece
        return degree * x - jnp.concatenate(sums, axis=1)

    poly = [jnp.concatenate([pg[t] for t in range(held)], axis=1)]
    poly.append(forward(poly[0]))
    for k in range(2, ORDER):
        poly.append(2.0 * forward(poly[-1]) - poly[-2])
    coarse_stack = jnp.concatenate(poly, axis=0).astype(BF16)
    coarse_pre = dot(conv_c[...], coarse_stack, ((0,), (0,)))
    coarse_gate = gate(coarse_pre)
    coarse_hidden = (coarse_pre * coarse_gate).astype(BF16)
    coarse_delta = (
        coarse_back * (coarse_gate * (1.0 + coarse_pre * (1.0 - coarse_gate)))
    ).astype(BF16)
    coarse_adj = dot(conv_c[...], coarse_delta)
    adj = [coarse_adj[32 * k : 32 * (k + 1)] for k in range(ORDER)]
    for k in range(ORDER - 1, 1, -1):
        adj[k - 1] = adj[k - 1] + 2.0 * adjoint(adj[k])
        adj[k - 2] = adj[k - 2] - adj[k]
    pooled_grad = (adj[0] + adjoint(adj[1]))[:, :LANES] * 0.0625

    pool_t = ((1,), (1,))
    grad_high, grad_low_part = split2(pooled_grad)
    raised = dot(jnp.concatenate([grad_high, grad_low_part], axis=0), pool[...], pool_t)
    fine_delta = ((direct + raised[:32] + raised[32:]) * fine_slope).astype(BF16)
    grad_fine = dot(fine_delta, stack[...], pool_t)

    pack[:, 0:48] = grad_fine[0:16]
    pack[:, 48:96] = grad_fine[16:32]
    pack[0:8, 96:128] = grad_top
    pack[8:16, 96:128] = jnp.zeros((8, 32), F32)
    if full:
        pair = push(pack, pack_in, rep_send.at[0], rep_recv.at[0], partner)

    span = slice(0, wide if full else LANES)
    gc[0:192, :] = dot(coarse_stack[:, span], coarse_delta[:, span], pool_t)
    gc[192:200, :] = dot(sig_high[:, span], coarse_hidden[:, span], pool_t) + dot(
        sig_low[:, span], coarse_hidden[:, span], pool_t)

    if full:
        pair.wait()
        total[0] = pack[...] + pack_in[...]
        spreads = []
        for p in peers:
            back = (held - p) % held
            spreads.append(
                push(total.at[0], total.at[back], all_send.at[p], all_recv.at[back], at(offsets[p])))
        pair_coarse = push(gc, gc_in, rep_send.at[1], rep_recv.at[1], partner)

    upward = dot(head_coarse, coarse_hidden[:, :LANES])
    up_high, up_low = split2(upward)
    result = result_fine + dot(up_high, pool[...], pool_t) + dot(up_low, pool[...], pool_t)
    pred[0] = result.astype(BF16)
    stores = [
        pltpu.make_async_copy(src, results[n], store_sem.at[n])
        for n, src in enumerate((pred, out_fine, out_coarse, out_head))
    ]
    stores[0].start()

    if full:
        pair_coarse.wait()
        sums = gc[...] + gc_in[...]
        out_coarse[...] = sums[0:192]
        stores[2].start()
        for copy in spreads:
            copy.wait()
        whole = total[0]
        for t in range(1, held):
            whole = whole + total[t]
    else:
        sums = gc[...]
        whole = pack[...]
        out_coarse[...] = sums[0:192]
        stores[2].start()
    out_fine[0:16, :] = whole[:, 0:48]
    out_fine[16:32, :] = whole[:, 48:96]
    out_head[:, 0:32] = whole[0:8, 96:128]
    out_head[:, 32:160] = sums[192:200]
    stores[1].start()
    stores[3].start()
    for copy in stores:
        copy.wait()


def write_out(*refs):
    copies = [pltpu.make_async_copy(refs[n], refs[4 + n], refs[8].at[n]) for n in range(4)]
    for copy in copies:
        copy.start()
    for copy in copies:
        copy.wait()


def on_device(ring, reps, *args):
    args = (*args[:5], args[5].T, args[6], args[7].T, args[8])
    sky, conv_f, conv_c, head = args[0], args[5], args[6], args[7]
    pixels = sky.shape[2]
    count = ring[0] * ring[1]
    full, held, _, _ = window_of(count)
    rows = (pixels // LANES + 2 * REACH) * 8
    scale = 1.0 / math.sqrt(pixels * count * sky.shape[0] * reps)
    dma = pltpu.SemaphoreType.DMA
    hbm = pl.BlockSpec(memory_space=pltpu.HBM)
    shapes = (
        jax.ShapeDtypeStruct(sky.shape, BF16),
        jax.ShapeDtypeStruct(conv_f.shape, F32),
        jax.ShapeDtypeStruct(conv_c.shape, F32),
        jax.ShapeDtypeStruct(head.shape, F32),
    )
    result = pl.pallas_call(
        partial(kernel, ring, reps, scale),
        out_shape=shapes,
        in_specs=[hbm] * 9,
        out_specs=(hbm,) * 4,
        scratch_shapes=[
            *[pltpu.VMEM(a.shape, a.dtype) for a in args],
            pltpu.VMEM((ORDER, rows, LANES), F32),
            pltpu.VMEM((rows, LANES), jnp.int32),
            pltpu.VMEM((rows, LANES), F32),
            pltpu.VMEM((8, rows, LANES), jnp.int32),
            pltpu.VMEM((8, rows, LANES), F32),
            pltpu.VMEM((rows, LANES), F32),
            pltpu.VMEM((ORDER * 8, pixels), BF16),
            pltpu.VMEM((pixels, pixels // 16), BF16),
            pltpu.VMEM((held, 24, LANES), F32),
            pltpu.VMEM((held, 32, LANES), F32),
            pltpu.VMEM((held // 2, 4 * LANES, 2 * LANES), BF16),
            pltpu.VMEM((200, LANES), F32),
            pltpu.VMEM((200, LANES), F32),
            pltpu.VMEM((16, LANES), F32),
            pltpu.VMEM((16, LANES), F32),
            pltpu.VMEM((held, 16, LANES), F32),
            pltpu.VMEM((8, LANES), F32),
            dma((6,)), dma((6,)),
            dma((held,)), dma((held,)),
            dma((held,)), dma((held,)),
            dma((2,)), dma((2,)),
            dma((held,)), dma((held,)),
            dma((9,)),
            *[pltpu.VMEM(r.shape, r.dtype) for r in shapes],
            dma((4,)),
        ],
        compiler_params=pltpu.CompilerParams(
            collective_id=0, has_side_effects=True, vmem_limit_bytes=VMEM_BYTES
        ),
        name="unet",
    )(*args)
    if full:
        result = pl.pallas_call(
            write_out,
            out_shape=shapes,
            in_specs=[hbm] * 4,
            out_specs=(hbm,) * 4,
            scratch_shapes=[dma((4,))],
            compiler_params=pltpu.CompilerParams(vmem_limit_bytes=VMEM_BYTES),
            name="write_out",
        )(*result)
    pred, grad_fine, grad_coarse, grad_head = result
    result = (pred, grad_fine.T, grad_coarse, grad_head.T)
    if not full:
        pred, grad_fine, grad_coarse, grad_head = result
        grads = lax.psum((grad_fine, grad_coarse, grad_head), ("patch", "sub", "rep"))
        result = (pred, *grads)
    return tuple(result)


def solution(mesh):
    pixel = P(None, ("patch", "sub"))
    maps = P(("parts", "rep"), None, ("patch", "sub"))
    ring = (mesh.shape["patch"], mesh.shape["sub"])
    return jax.shard_map(
        partial(on_device, ring, mesh.shape["rep"]),
        mesh=mesh,
        in_specs=(maps, pixel, pixel, pixel, pixel, P(), P(), P(), maps),
        out_specs=(maps, P("parts", None), P("parts", None), P("parts", None)),
        check_vma=False,
    )
```

```python
from functools import partial
import math

import jax
import jax.numpy as jnp
from jax import lax
from jax.experimental import pallas as pl
from jax.experimental.pallas import tpu as pltpu
from jax.sharding import PartitionSpec as P

ORDER = 6
LANES = 128
REACH = ORDER - 1
VMEM_BYTES = 64 * 1024 * 1024
MESH = pl.DeviceIdType.MESH
F32 = jnp.float32
BF16 = jnp.bfloat16


def dot(a, b, dims=((1,), (0,))):
    return lax.dot_general(a, b, (dims, ((), ())), preferred_element_type=F32)


def split2(x):
    high = x.astype(BF16)
    low = (x - high.astype(F32)).astype(BF16)
    return high, low


def gate(v):
    return 0.5 * jnp.tanh(0.5 * v) + 0.5


def window_of(count):
    full = count <= 4 * REACH + 2
    held = count if full else 4 * REACH + 2
    offsets = [d if d <= held // 2 else d - held for d in range(held)]
    peers = [p for p in range(1, held) if full or abs(offsets[p]) <= 2 * REACH]
    return full, held, offsets, peers


def kernel(
    ring, reps, scale, *refs
):
    hbm = refs[:9]
    results = refs[9:13]
    local = refs[13:22]
    sky, nbf, wf, nbc, wc, conv_f, conv_c, head, cot = local
    (
    field, nb, wt, idx8, w8, deg, stack, pool, cg, pg, mat, gc, gc_in, pack, pack_in, total, halo_out, halo_in,
    halo_send, halo_recv, cg_send, cg_recv, pg_send, pg_recv, rep_send, rep_recv, all_send, all_recv,
        load_sem, pred, out_fine, out_coarse, out_head, store_sem,
    ) = refs[22:]
    loads = [
        pltpu.make_async_copy(hbm[n], local[n], load_sem.at[n]) for n in range(9)
    ]
    for n in (0, 1, 2, 8, 3, 4, 5, 7, 6):
        loads[n].start()
    patches, subs = ring
    count = patches * subs
    full, held, offsets, peers = window_of(count)
    me = lax.axis_index("patch") * subs + lax.axis_index("sub")
    rep = lax.axis_index("rep")
    blocks = sky.shape[2] // LANES
    first, last = REACH, REACH + blocks

    def at(d):
        q = lax.rem(me + (d % count), count)
        return {"patch": lax.div(q, subs), "sub": lax.rem(q, subs)}

    partner = {"rep": lax.rem(rep + 1, reps)}
    barrier = pltpu.get_barrier_semaphore()
    for p in peers:
        pl.semaphore_signal(barrier, inc=1, device_id=at(offsets[p]), device_id_type=MESH)
    if full:
        pl.semaphore_signal(barrier, inc=1, device_id=partner, device_id_type=MESH)

    for n in range(3):
        loads[n].wait()
    for b in range(blocks):
        rows = slice((first + b) * 8, (first + b + 1) * 8)
        lanes = slice(b * LANES, (b + 1) * LANES)
        field[0, rows, :] = sky[0, :, lanes].astype(F32)
        nb[rows, :] = nbf[:, lanes]
        wt[rows, :] = wf[:, lanes] * 0.125

    pl.semaphore_wait(barrier, len(peers) + (1 if full else 0))

    def push(src, dst, ssem, rsem, to):
        copy = pltpu.make_async_remote_copy(
            src_ref=src, dst_ref=dst, send_sem=ssem, recv_sem=rsem, device_id=to, device_id_type=MESH
        )
        copy.start()
        return copy

    def ends(b0):
        inner = slice((b0 if b0 == first else b0 + 1) * 8, (b0 + REACH - (b0 == first)) * 8)
        return jnp.concatenate([
            field[0, slice(b0 * 8, (b0 + REACH) * 8), :], jnp.zeros((8, LANES), F32),
            nb[inner, :].astype(F32), wt[inner, :]], axis=0).astype(BF16)

    halo_out[0] = ends(last - REACH)
    halo_out[1] = ends(first)
    halos = [
        push(halo_out.at[n], halo_in.at[n], halo_send.at[n], halo_recv.at[n], at(1 - 2 * n))
        for n in range(2)
    ]

    pixel = lax.broadcasted_iota(jnp.int32, pool.shape, 0)
    coarse = lax.broadcasted_iota(jnp.int32, pool.shape, 1)
    pool[...] = jnp.where((pixel >> 4) == coarse, 1.0, 0.0).astype(BF16)
    for n in (8, 3, 4):
        loads[n].wait()
    signal = (cot[0].astype(F32) * scale).astype(BF16)
    pooled_signal = dot(signal, pool[...])
    cg[0] = jnp.concatenate([
        nbc[...].astype(F32), wc[...] * 0.125, pooled_signal,
        pooled_signal - pooled_signal.astype(BF16).astype(F32)], axis=0).astype(BF16)

    def spread_slots(b0, b1):
        shape = (b1 - b0, 8, LANES)
        rows = slice(b0 * 8, b1 * 8)
        lane = lax.broadcasted_iota(jnp.int32, ((b1 - b0) * 8, LANES), 1)
        near_nb = nb[rows, :].reshape(shape)
        near_w = wt[rows, :].reshape(shape)
        acc = None
        for j in range(8):
            offs = jnp.broadcast_to(near_nb[:, j : j + 1, :], shape).reshape((b1 - b0) * 8, LANES)
            wide = jnp.broadcast_to(near_w[:, j : j + 1, :], shape).reshape((b1 - b0) * 8, LANES)
            idx8[j, rows, :] = offs + lane
            w8[j, rows, :] = wide
            acc = wide if acc is None else acc + wide
        deg[rows, :] = acc - 1.0

    def level(k, b0, b1):
        rows = slice(b0 * 8, b1 * 8)
        lo = field[k - 1, slice(b0 * 8 - 8, b1 * 8 - 8), :]
        mid = field[k - 1, rows, :]
        hi = field[k - 1, slice(b0 * 8 + 8, b1 * 8 + 8), :]
        near = None
        for j in range(8):
            index = idx8[j, rows, :]
            source = index & (LANES - 1)
            g = jnp.where(
                index < 0,
                jnp.take_along_axis(lo, source, axis=1, mode="promise_in_bounds"),
                jnp.where(
                    index >= LANES,
                    jnp.take_along_axis(hi, source, axis=1, mode="promise_in_bounds"),
                    jnp.take_along_axis(mid, source, axis=1, mode="promise_in_bounds"),
                ),
            )
            term = w8[j, rows, :] * g
            near = term if near is None else near + term
        lap = deg[rows, :] * mid - near
        field[k, rows, :] = lap if k == 1 else 2.0 * lap - field[k - 2, rows, :]

    spread_slots(first, last)
    for k in range(1, ORDER):
        level(k, first + k, last - k)
    for copy in halos:
        copy.wait()
    gathers = []
    for p in peers:
        back = (held - p) % held
        gathers.append(push(cg.at[0], cg.at[back], cg_send.at[p], cg_recv.at[back], at(offsets[p])))
    for n, (b0, skip) in enumerate(((0, 1), (last, 0))):
        got = halo_in[n].astype(F32)
        inner = slice((b0 + skip) * 8, (b0 + skip + REACH - 1) * 8)
        field[0, slice(b0 * 8, (b0 + REACH) * 8), :] = got[: REACH * 8]
        nb[inner, :] = got[48:80].astype(jnp.int32)
        wt[inner, :] = got[80:112]
    spread_slots(1, first)
    spread_slots(last, last + REACH - 1)
    for k in range(1, ORDER):
        level(k, k, first + k)
        level(k, last - k, last + REACH - k)
    for b in range(blocks):
        tile = field[:, slice((first + b) * 8, (first + b + 1) * 8), :]
        stack[:, slice(b * LANES, (b + 1) * LANES)] = tile.reshape(ORDER * 8, LANES).astype(BF16)

    for n in (5, 6, 7):
        loads[n].wait()
    fine_pre = dot(conv_f[...], stack[...])
    fine_gate = gate(fine_pre)
    hidden = (fine_pre * fine_gate).astype(BF16)
    pg[0] = (dot(hidden, pool[...]) * 0.0625).astype(BF16)
    pooled_gathers = []
    for p in peers:
        back = (held - p) % held
        pooled_gathers.append(
            push(pg.at[0], pg.at[back], pg_send.at[p], pg_recv.at[back], at(offsets[p])))

    grad_top = dot(signal, hidden, ((1,), (1,)))
    fine_slope = fine_gate * (1.0 + fine_pre * (1.0 - fine_gate))
    head_fine = head[:, 0:32]
    head_coarse = head[:, 32:160]
    direct = dot(head_fine, signal, ((0,), (0,)))
    result_fine = dot(head_fine, hidden)

    for copy in gathers:
        copy.wait()
    if not full:
        cg[held // 2] = cg[0]
    source = lax.broadcasted_iota(jnp.int32, (3 * LANES, LANES), 0)
    lane = lax.broadcasted_iota(jnp.int32, (8, LANES), 1)
    degrees, signals = [], []
    for t in range(held):
        tables = cg[t].astype(F32)
        offs = tables[0:8].astype(jnp.int32) + lane + LANES
        weight = tables[8:16]
        block = None
        for j in range(8):
            term = jnp.where(offs[j : j + 1, :] == source, weight[j : j + 1, :], 0.0)
            block = term if block is None else block + term
        u, side = t // 2, t % 2
        cols = slice(side * LANES, (side + 1) * LANES)
        mat[u, slice(side * LANES, (side + 3) * LANES), cols] = block.astype(BF16)
        empty = 3 * LANES if side == 0 else 0
        mat[u, slice(empty, empty + LANES), cols] = jnp.zeros((LANES, LANES), BF16)
        degrees.append(jnp.sum(weight, axis=0, keepdims=True) - 1.0)
        signals.append(tables[16:32])
    degree = jnp.concatenate(degrees, axis=1)
    signals = jnp.concatenate(signals, axis=1)
    sig_high, sig_low = signals[0:8].astype(BF16), signals[8:16].astype(BF16)
    coarse_back = dot(head_coarse, sig_high, ((0,), (0,))) + dot(head_coarse, sig_low, ((0,), (0,)))

    for copy in pooled_gathers:
        copy.wait()
    if not full:
        pg[held // 2] = pg[0]

    wide = held * LANES

    def forward(x):
        rows = x.shape[0]
        high, low = split2(x)
        both = jnp.concatenate([high, low], axis=0)
        both = jnp.concatenate([both[:, wide - LANES :], both, both[:, :LANES]], axis=1)
        parts = []
        for u in range(held // 2):
            got = dot(both[:, 2 * u * LANES : (2 * u + 4) * LANES], mat[u])
            parts.append(got[:rows] + got[rows:])
        return degree * x - jnp.concatenate(parts, axis=1)

    def adjoint(x):
        rows = x.shape[0]
        high, low = split2(x)
        both = jnp.concatenate([high, low], axis=0)
        sums = [None] * held
        for u in range(held // 2):
            got = dot(both[:, 2 * u * LANES : (2 * u + 2) * LANES], mat[u], ((1,), (1,)))
            got = got[:rows] + got[rows:]
            for i in range(4):
                s = (2 * u - 1 + i) % held
                piece = got[:, i * LANES : (i + 1) * LANES]
                sums[s] = piece if sums[s] is None else sums[s] + piece
        return degree * x - jnp.concatenate(sums, axis=1)

    poly = [jnp.concatenate([pg[t] for t in range(held)], axis=1).astype(F32)]
    poly.append(forward(poly[0]))
    for k in range(2, ORDER):
        poly.append(2.0 * forward(poly[-1]) - poly[-2])
    coarse_stack = jnp.concatenate(poly, axis=0).astype(BF16)
    coarse_pre = dot(conv_c[...], coarse_stack, ((0,), (0,)))
    coarse_gate = gate(coarse_pre)
    coarse_hidden = (coarse_pre * coarse_gate).astype(BF16)
    coarse_delta = (
        coarse_back * (coarse_gate * (1.0 + coarse_pre * (1.0 - coarse_gate)))
    ).astype(BF16)
    coarse_adj = dot(conv_c[...], coarse_delta)
    adj = [coarse_adj[32 * k : 32 * (k + 1)] for k in range(ORDER)]
    for k in range(ORDER - 1, 1, -1):
        adj[k - 1] = adj[k - 1] + 2.0 * adjoint(adj[k])
        adj[k - 2] = adj[k - 2] - adj[k]
    pooled_grad = (adj[0] + adjoint(adj[1]))[:, :LANES] * 0.0625

    pool_t = ((1,), (1,))
    grad_high, grad_low_part = split2(pooled_grad)
    raised = dot(jnp.concatenate([grad_high, grad_low_part], axis=0), pool[...], pool_t)
    fine_delta = ((direct + raised[:32] + raised[32:]) * fine_slope).astype(BF16)
    grad_fine = dot(fine_delta, stack[...], pool_t)

    pack[:, 0:48] = grad_fine[0:16]
    pack[:, 48:96] = grad_fine[16:32]
    pack[0:8, 96:128] = grad_top
    pack[8:16, 96:128] = jnp.zeros((8, 32), F32)
    if full:
        pair = push(pack, pack_in, rep_send.at[0], rep_recv.at[0], partner)

    span = slice(0, wide if full else LANES)
    gc[0:192, :] = dot(coarse_stack[:, span], coarse_delta[:, span], pool_t)
    gc[192:200, :] = dot(sig_high[:, span], coarse_hidden[:, span], pool_t) + dot(
        sig_low[:, span], coarse_hidden[:, span], pool_t)

    if full:
        pair_coarse = push(gc, gc_in, rep_send.at[1], rep_recv.at[1], partner)
        pair.wait()
        total[0] = (pack[...] + pack_in[...]).astype(BF16)
        spreads = []
        for p in peers:
            back = (held - p) % held
            spreads.append(
                push(total.at[0], total.at[back], all_send.at[p], all_recv.at[back], at(offsets[p])))

    upward = dot(head_coarse, coarse_hidden[:, :LANES])
    up_high, up_low = split2(upward)
    result = result_fine + dot(up_high, pool[...], pool_t) + dot(up_low, pool[...], pool_t)
    pred[0] = result.astype(BF16)
    stores = [
        pltpu.make_async_copy(src, results[n], store_sem.at[n])
        for n, src in enumerate((pred, out_fine, out_coarse, out_head))
    ]
    stores[0].start()

    if full:
        pair_coarse.wait()
        sums = gc[...] + gc_in[...]
        out_coarse[...] = sums[0:192]
        stores[2].start()
        for copy in spreads:
            copy.wait()
        whole = total[0].astype(F32)
        for t in range(1, held):
            whole = whole + total[t].astype(F32)
    else:
        sums = gc[...]
        whole = pack[...]
        out_coarse[...] = sums[0:192]
        stores[2].start()
    out_fine[0:16, :] = whole[:, 0:48]
    out_fine[16:32, :] = whole[:, 48:96]
    out_head[:, 0:32] = whole[0:8, 96:128]
    out_head[:, 32:160] = sums[192:200]
    stores[1].start()
    stores[3].start()
    for copy in stores:
        copy.wait()


def write_out(*refs):
    held, sems = refs[8:12], refs[12]
    loads = [pltpu.make_async_copy(refs[n], held[n], sems.at[n]) for n in range(4)]
    stores = [pltpu.make_async_copy(held[n], refs[4 + n], sems.at[4 + n]) for n in range(4)]
    for copy in loads:
        copy.start()
    for load, store in zip(loads, stores):
        load.wait()
        store.start()
    for copy in stores:
        copy.wait()


def on_device(ring, reps, *args):
    args = (*args[:5], args[5].T, args[6], args[7].T, args[8])
    sky, conv_f, conv_c, head = args[0], args[5], args[6], args[7]
    pixels = sky.shape[2]
    count = ring[0] * ring[1]
    full, held, _, _ = window_of(count)
    rows = (pixels // LANES + 2 * REACH) * 8
    scale = 1.0 / math.sqrt(pixels * count * sky.shape[0] * reps)
    dma = pltpu.SemaphoreType.DMA
    hbm = pl.BlockSpec(memory_space=pltpu.HBM)
    shapes = (
        jax.ShapeDtypeStruct(sky.shape, BF16),
        jax.ShapeDtypeStruct(conv_f.shape, F32),
        jax.ShapeDtypeStruct(conv_c.shape, F32),
        jax.ShapeDtypeStruct(head.shape, F32),
    )
    result = pl.pallas_call(
        partial(kernel, ring, reps, scale),
        out_shape=shapes,
        in_specs=[hbm] * 9,
        out_specs=(hbm,) * 4,
        scratch_shapes=[
            *[pltpu.VMEM(a.shape, a.dtype) for a in args],
            pltpu.VMEM((ORDER, rows, LANES), F32),
            pltpu.VMEM((rows, LANES), jnp.int32),
            pltpu.VMEM((rows, LANES), F32),
            pltpu.VMEM((8, rows, LANES), jnp.int32),
            pltpu.VMEM((8, rows, LANES), F32),
            pltpu.VMEM((rows, LANES), F32),
            pltpu.VMEM((ORDER * 8, pixels), BF16),
            pltpu.VMEM((pixels, pixels // 16), BF16),
            pltpu.VMEM((held, 32, LANES), BF16),
            pltpu.VMEM((held, 32, LANES), BF16),
            pltpu.VMEM((held // 2, 4 * LANES, 2 * LANES), BF16),
            pltpu.VMEM((200, LANES), F32),
            pltpu.VMEM((200, LANES), F32),
            pltpu.VMEM((16, LANES), F32),
            pltpu.VMEM((16, LANES), F32),
            pltpu.VMEM((held, 16, LANES), BF16),
            pltpu.VMEM((2, 112, LANES), BF16),
            pltpu.VMEM((2, 112, LANES), BF16),
            dma((2,)), dma((2,)),
            dma((held,)), dma((held,)),
            dma((held,)), dma((held,)),
            dma((2,)), dma((2,)),
            dma((held,)), dma((held,)),
            dma((9,)),
            *[pltpu.VMEM(r.shape, r.dtype) for r in shapes],
            dma((4,)),
        ],
        compiler_params=pltpu.CompilerParams(
            collective_id=0, has_side_effects=True, vmem_limit_bytes=VMEM_BYTES
        ),
        name="unet",
    )(*args)
    if full:
        result = pl.pallas_call(
            write_out,
            out_shape=shapes,
            in_specs=[hbm] * 4,
            out_specs=(hbm,) * 4,
            scratch_shapes=[*[pltpu.VMEM(r.shape, r.dtype) for r in shapes], dma((8,))],
            compiler_params=pltpu.CompilerParams(vmem_limit_bytes=VMEM_BYTES),
            name="write_out",
        )(*result)
    pred, grad_fine, grad_coarse, grad_head = result
    result = (pred, grad_fine.T, grad_coarse, grad_head.T)
    if not full:
        pred, grad_fine, grad_coarse, grad_head = result
        grads = lax.psum((grad_fine, grad_coarse, grad_head), ("patch", "sub", "rep"))
        result = (pred, *grads)
    return tuple(result)


def solution(mesh):
    pixel = P(None, ("patch", "sub"))
    maps = P(("parts", "rep"), None, ("patch", "sub"))
    ring = (mesh.shape["patch"], mesh.shape["sub"])
    return jax.shard_map(
        partial(on_device, ring, mesh.shape["rep"]),
        mesh=mesh,
        in_specs=(maps, pixel, pixel, pixel, pixel, P(), P(), P(), maps),
        out_specs=(maps, P("parts", None), P("parts", None), P("parts", None)),
        check_vma=False,
    )
```

```python
from functools import partial
import math

import jax
import jax.numpy as jnp
from jax import lax
from jax.experimental import pallas as pl
from jax.experimental.pallas import tpu as pltpu
from jax.sharding import PartitionSpec as P

ORDER = 6
LANES = 128
REACH = ORDER - 1
VMEM_BYTES = 64 * 1024 * 1024
MESH = pl.DeviceIdType.MESH
F32 = jnp.float32
BF16 = jnp.bfloat16


def dot(a, b, dims=((1,), (0,))):
    return lax.dot_general(a, b, (dims, ((), ())), preferred_element_type=F32)


def split2(x):
    high = x.astype(BF16)
    low = (x - high.astype(F32)).astype(BF16)
    return high, low


def gate(v):
    return 0.5 * jnp.tanh(0.5 * v) + 0.5


def window_of(count):
    full = count <= 4 * REACH + 2
    held = count if full else 4 * REACH + 2
    offsets = [d if d <= held // 2 else d - held for d in range(held)]
    peers = [p for p in range(1, held) if full or abs(offsets[p]) <= 2 * REACH]
    return full, held, offsets, peers


def kernel(
    ring, reps, scale, *refs
):
    hbm = refs[:9]
    results = refs[9:13]
    local = refs[13:22]
    sky, nbf, wf, nbc, wc, conv_f, conv_c, head, cot = local
    (
    field, nb, wt, idx8, w8, deg, stack, pool, cg, pg, mat, gc, gc_in, pack, pack_in, total, halo_out, halo_in,
    halo_send, halo_recv, cg_send, cg_recv, pg_send, pg_recv, rep_send, rep_recv, all_send, all_recv,
        load_sem, pred, out_fine, out_coarse, out_head, store_sem,
    ) = refs[22:]
    loads = [
        pltpu.make_async_copy(hbm[n], local[n], load_sem.at[n]) for n in range(9)
    ]
    for n in (0, 1, 2, 8, 3, 4, 5, 7, 6):
        loads[n].start()
    patches, subs = ring
    count = patches * subs
    full, held, offsets, peers = window_of(count)
    me = lax.axis_index("patch") * subs + lax.axis_index("sub")
    rep = lax.axis_index("rep")
    blocks = sky.shape[2] // LANES
    first, last = REACH, REACH + blocks

    def at(d):
        q = lax.rem(me + (d % count), count)
        return {"patch": lax.div(q, subs), "sub": lax.rem(q, subs)}

    partner = {"rep": lax.rem(rep + 1, reps)}
    barrier = pltpu.get_barrier_semaphore()
    for p in peers:
        pl.semaphore_signal(barrier, inc=1, device_id=at(offsets[p]), device_id_type=MESH)
    if full:
        pl.semaphore_signal(barrier, inc=1, device_id=partner, device_id_type=MESH)

    for n in range(3):
        loads[n].wait()
    for b in range(blocks):
        rows = slice((first + b) * 8, (first + b + 1) * 8)
        lanes = slice(b * LANES, (b + 1) * LANES)
        field[0, rows, :] = sky[0, :, lanes].astype(F32)
        nb[rows, :] = nbf[:, lanes]
        wt[rows, :] = wf[:, lanes] * 0.125

    pl.semaphore_wait(barrier, len(peers) + (1 if full else 0))

    def push(src, dst, ssem, rsem, to):
        copy = pltpu.make_async_remote_copy(
            src_ref=src, dst_ref=dst, send_sem=ssem, recv_sem=rsem, device_id=to, device_id_type=MESH
        )
        copy.start()
        return copy

    def ends(b0):
        inner = slice((b0 if b0 == first else b0 + 1) * 8, (b0 + REACH - (b0 == first)) * 8)
        return jnp.concatenate([
            field[0, slice(b0 * 8, (b0 + REACH) * 8), :], jnp.zeros((8, LANES), F32),
            nb[inner, :].astype(F32), wt[inner, :]], axis=0).astype(BF16)

    halo_out[0] = ends(last - REACH)
    halo_out[1] = ends(first)
    halos = [
        push(halo_out.at[n], halo_in.at[n], halo_send.at[n], halo_recv.at[n], at(1 - 2 * n))
        for n in range(2)
    ]

    pixel = lax.broadcasted_iota(jnp.int32, pool.shape, 0)
    coarse = lax.broadcasted_iota(jnp.int32, pool.shape, 1)
    pool[...] = jnp.where((pixel >> 4) == coarse, 1.0, 0.0).astype(BF16)
    for n in (8, 3, 4):
        loads[n].wait()
    signal = (cot[0].astype(F32) * scale).astype(BF16)
    pooled_signal = dot(signal, pool[...])
    cg[0] = jnp.concatenate([
        nbc[...].astype(F32), wc[...] * 0.125, pooled_signal,
        pooled_signal - pooled_signal.astype(BF16).astype(F32)], axis=0).astype(BF16)

    gathers = []
    for p in peers:
        back = (held - p) % held
        gathers.append(push(cg.at[0], cg.at[back], cg_send.at[p], cg_recv.at[back], at(offsets[p])))

    def spread_slots(b0, b1):
        shape = (b1 - b0, 8, LANES)
        rows = slice(b0 * 8, b1 * 8)
        lane = lax.broadcasted_iota(jnp.int32, ((b1 - b0) * 8, LANES), 1)
        near_nb = nb[rows, :].reshape(shape)
        near_w = wt[rows, :].reshape(shape)
        acc = None
        for j in range(8):
            offs = jnp.broadcast_to(near_nb[:, j : j + 1, :], shape).reshape((b1 - b0) * 8, LANES)
            wide = jnp.broadcast_to(near_w[:, j : j + 1, :], shape).reshape((b1 - b0) * 8, LANES)
            idx8[j, rows, :] = offs + lane
            w8[j, rows, :] = wide
            acc = wide if acc is None else acc + wide
        deg[rows, :] = acc - 1.0

    def level(k, b0, b1):
        rows = slice(b0 * 8, b1 * 8)
        lo = field[k - 1, slice(b0 * 8 - 8, b1 * 8 - 8), :]
        mid = field[k - 1, rows, :]
        hi = field[k - 1, slice(b0 * 8 + 8, b1 * 8 + 8), :]
        near = None
        for j in range(8):
            index = idx8[j, rows, :]
            source = index & (LANES - 1)
            g = jnp.where(
                index < 0,
                jnp.take_along_axis(lo, source, axis=1, mode="promise_in_bounds"),
                jnp.where(
                    index >= LANES,
                    jnp.take_along_axis(hi, source, axis=1, mode="promise_in_bounds"),
                    jnp.take_along_axis(mid, source, axis=1, mode="promise_in_bounds"),
                ),
            )
            term = w8[j, rows, :] * g
            near = term if near is None else near + term
        lap = deg[rows, :] * mid - near
        field[k, rows, :] = lap if k == 1 else 2.0 * lap - field[k - 2, rows, :]

    spread_slots(first, last)
    for k in range(1, ORDER):
        level(k, first + k, last - k)
    for copy in halos:
        copy.wait()
    for n, (b0, skip) in enumerate(((0, 1), (last, 0))):
        got = halo_in[n].astype(F32)
        inner = slice((b0 + skip) * 8, (b0 + skip + REACH - 1) * 8)
        field[0, slice(b0 * 8, (b0 + REACH) * 8), :] = got[: REACH * 8]
        nb[inner, :] = got[48:80].astype(jnp.int32)
        wt[inner, :] = got[80:112]
    spread_slots(1, first)
    spread_slots(last, last + REACH - 1)
    for k in range(1, ORDER):
        level(k, k, first + k)
        level(k, last - k, last + REACH - k)
    for b in range(blocks):
        tile = field[:, slice((first + b) * 8, (first + b + 1) * 8), :]
        stack[:, slice(b * LANES, (b + 1) * LANES)] = tile.reshape(ORDER * 8, LANES).astype(BF16)

    for n in (5, 6, 7):
        loads[n].wait()
    fine_pre = dot(conv_f[...], stack[...])
    fine_gate = gate(fine_pre)
    hidden = (fine_pre * fine_gate).astype(BF16)
    pg[0] = (dot(hidden, pool[...]) * 0.0625).astype(BF16)
    pooled_gathers = []
    for p in peers:
        back = (held - p) % held
        pooled_gathers.append(
            push(pg.at[0], pg.at[back], pg_send.at[p], pg_recv.at[back], at(offsets[p])))

    grad_top = dot(signal, hidden, ((1,), (1,)))
    fine_slope = fine_gate * (1.0 + fine_pre * (1.0 - fine_gate))
    head_fine = head[:, 0:32]
    head_coarse = head[:, 32:160]
    direct = dot(head_fine, signal, ((0,), (0,)))
    result_fine = dot(head_fine, hidden)

    for copy in gathers:
        copy.wait()
    if not full:
        cg[held // 2] = cg[0]
    source = lax.broadcasted_iota(jnp.int32, (3 * LANES, LANES), 0)
    lane = lax.broadcasted_iota(jnp.int32, (8, LANES), 1)
    degrees, signals = [], []
    for t in range(held):
        tables = cg[t].astype(F32)
        offs = tables[0:8].astype(jnp.int32) + lane + LANES
        weight = tables[8:16]
        block = None
        for j in range(8):
            term = jnp.where(offs[j : j + 1, :] == source, weight[j : j + 1, :], 0.0)
            block = term if block is None else block + term
        u, side = t // 2, t % 2
        cols = slice(side * LANES, (side + 1) * LANES)
        mat[u, slice(side * LANES, (side + 3) * LANES), cols] = block.astype(BF16)
        empty = 3 * LANES if side == 0 else 0
        mat[u, slice(empty, empty + LANES), cols] = jnp.zeros((LANES, LANES), BF16)
        degrees.append(jnp.sum(weight, axis=0, keepdims=True) - 1.0)
        signals.append(tables[16:32])
    degree = jnp.concatenate(degrees, axis=1)
    signals = jnp.concatenate(signals, axis=1)
    sig_high, sig_low = signals[0:8].astype(BF16), signals[8:16].astype(BF16)
    coarse_back = dot(head_coarse, sig_high, ((0,), (0,))) + dot(head_coarse, sig_low, ((0,), (0,)))

    for copy in pooled_gathers:
        copy.wait()
    if not full:
        pg[held // 2] = pg[0]

    wide = held * LANES

    def forward(x):
        both = x.astype(BF16)
        both = jnp.concatenate([both[:, wide - LANES :], both, both[:, :LANES]], axis=1)
        parts = []
        for u in range(held // 2):
            parts.append(dot(both[:, 2 * u * LANES : (2 * u + 4) * LANES], mat[u]))
        return degree * x - jnp.concatenate(parts, axis=1)

    def adjoint(x, reach):
        both = x.astype(BF16)
        sums = [None] * held
        for u in range(held // 2):
            if all(abs(offsets[(2 * u - 1 + i) % held]) > reach for i in range(4)):
                continue
            got = dot(both[:, 2 * u * LANES : (2 * u + 2) * LANES], mat[u], ((1,), (1,)))
            for i in range(4):
                s = (2 * u - 1 + i) % held
                piece = got[:, i * LANES : (i + 1) * LANES]
                sums[s] = piece if sums[s] is None else sums[s] + piece
        blank = jnp.zeros((x.shape[0], LANES), F32)
        return degree * x - jnp.concatenate([blank if s is None else s for s in sums], axis=1)

    poly = [jnp.concatenate([pg[t] for t in range(held)], axis=1).astype(F32)]
    poly.append(forward(poly[0]))
    for k in range(2, ORDER):
        poly.append(2.0 * forward(poly[-1]) - poly[-2])
    coarse_stack = jnp.concatenate(poly, axis=0).astype(BF16)
    coarse_pre = dot(conv_c[...], coarse_stack, ((0,), (0,)))
    coarse_gate = gate(coarse_pre)
    coarse_hidden = (coarse_pre * coarse_gate).astype(BF16)
    coarse_delta = (
        coarse_back * (coarse_gate * (1.0 + coarse_pre * (1.0 - coarse_gate)))
    ).astype(BF16)
    coarse_adj = dot(conv_c[...], coarse_delta)
    adj = [coarse_adj[32 * k : 32 * (k + 1)] for k in range(ORDER)]
    for k in range(ORDER - 1, 1, -1):
        adj[k - 1] = adj[k - 1] + 2.0 * adjoint(adj[k], k - 1)
        adj[k - 2] = adj[k - 2] - adj[k]
    pooled_grad = (adj[0] + adjoint(adj[1], 0))[:, :LANES] * 0.0625

    pool_t = ((1,), (1,))
    grad_high, grad_low_part = split2(pooled_grad)
    raised = dot(jnp.concatenate([grad_high, grad_low_part], axis=0), pool[...], pool_t)
    fine_delta = ((direct + raised[:32] + raised[32:]) * fine_slope).astype(BF16)
    grad_fine = dot(fine_delta, stack[...], pool_t)

    pack[:, 0:48] = grad_fine[0:16]
    pack[:, 48:96] = grad_fine[16:32]
    pack[0:8, 96:128] = grad_top
    pack[8:16, 96:128] = jnp.zeros((8, 32), F32)
    if full:
        pair = push(pack, pack_in, rep_send.at[0], rep_recv.at[0], partner)

    span = slice(0, wide if full else LANES)
    gc[0:192, :] = dot(coarse_stack[:, span], coarse_delta[:, span], pool_t)
    gc[192:200, :] = dot(sig_high[:, span], coarse_hidden[:, span], pool_t) + dot(
        sig_low[:, span], coarse_hidden[:, span], pool_t)

    if full:
        pair_coarse = push(gc, gc_in, rep_send.at[1], rep_recv.at[1], partner)
        pair.wait()
        total[0] = (pack[...] + pack_in[...]).astype(BF16)
        spreads = []
        for p in peers:
            back = (held - p) % held
            spreads.append(
                push(total.at[0], total.at[back], all_send.at[p], all_recv.at[back], at(offsets[p])))

    upward = dot(head_coarse, coarse_hidden[:, :LANES])
    up_high, up_low = split2(upward)
    result = result_fine + dot(up_high, pool[...], pool_t) + dot(up_low, pool[...], pool_t)
    pred[0] = result.astype(BF16)
    stores = [
        pltpu.make_async_copy(src, results[n], store_sem.at[n])
        for n, src in enumerate((pred, out_fine, out_coarse, out_head))
    ]
    stores[0].start()

    if full:
        pair_coarse.wait()
        sums = gc[...] + gc_in[...]
        out_coarse[...] = sums[0:192]
        stores[2].start()
        for copy in spreads:
            copy.wait()
        whole = total[0].astype(F32)
        for t in range(1, held):
            whole = whole + total[t].astype(F32)
    else:
        sums = gc[...]
        whole = pack[...]
        out_coarse[...] = sums[0:192]
        stores[2].start()
    out_fine[0:16, :] = whole[:, 0:48]
    out_fine[16:32, :] = whole[:, 48:96]
    out_head[:, 0:32] = whole[0:8, 96:128]
    out_head[:, 32:160] = sums[192:200]
    stores[1].start()
    stores[3].start()
    for copy in stores:
        copy.wait()


def write_out(*refs):
    held, sems = refs[8:12], refs[12]
    loads = [pltpu.make_async_copy(refs[n], held[n], sems.at[n]) for n in range(4)]
    stores = [pltpu.make_async_copy(held[n], refs[4 + n], sems.at[4 + n]) for n in range(4)]
    for copy in loads:
        copy.start()
    for load, store in zip(loads, stores):
        load.wait()
        store.start()
    for copy in stores:
        copy.wait()


def on_device(ring, reps, *args):
    args = (*args[:5], args[5].T, args[6], args[7].T, args[8])
    sky, conv_f, conv_c, head = args[0], args[5], args[6], args[7]
    pixels = sky.shape[2]
    count = ring[0] * ring[1]
    full, held, _, _ = window_of(count)
    rows = (pixels // LANES + 2 * REACH) * 8
    scale = 1.0 / math.sqrt(pixels * count * sky.shape[0] * reps)
    dma = pltpu.SemaphoreType.DMA
    hbm = pl.BlockSpec(memory_space=pltpu.HBM)
    shapes = (
        jax.ShapeDtypeStruct(sky.shape, BF16),
        jax.ShapeDtypeStruct(conv_f.shape, F32),
        jax.ShapeDtypeStruct(conv_c.shape, F32),
        jax.ShapeDtypeStruct(head.shape, F32),
    )
    result = pl.pallas_call(
        partial(kernel, ring, reps, scale),
        out_shape=shapes,
        in_specs=[hbm] * 9,
        out_specs=(hbm,) * 4,
        scratch_shapes=[
            *[pltpu.VMEM(a.shape, a.dtype) for a in args],
            pltpu.VMEM((ORDER, rows, LANES), F32),
            pltpu.VMEM((rows, LANES), jnp.int32),
            pltpu.VMEM((rows, LANES), F32),
            pltpu.VMEM((8, rows, LANES), jnp.int32),
            pltpu.VMEM((8, rows, LANES), F32),
            pltpu.VMEM((rows, LANES), F32),
            pltpu.VMEM((ORDER * 8, pixels), BF16),
            pltpu.VMEM((pixels, pixels // 16), BF16),
            pltpu.VMEM((held, 32, LANES), BF16),
            pltpu.VMEM((held, 32, LANES), BF16),
            pltpu.VMEM((held // 2, 4 * LANES, 2 * LANES), BF16),
            pltpu.VMEM((200, LANES), F32),
            pltpu.VMEM((200, LANES), F32),
            pltpu.VMEM((16, LANES), F32),
            pltpu.VMEM((16, LANES), F32),
            pltpu.VMEM((held, 16, LANES), BF16),
            pltpu.VMEM((2, 112, LANES), BF16),
            pltpu.VMEM((2, 112, LANES), BF16),
            dma((2,)), dma((2,)),
            dma((held,)), dma((held,)),
            dma((held,)), dma((held,)),
            dma((2,)), dma((2,)),
            dma((held,)), dma((held,)),
            dma((9,)),
            *[pltpu.VMEM(r.shape, r.dtype) for r in shapes],
            dma((4,)),
        ],
        compiler_params=pltpu.CompilerParams(
            collective_id=0, has_side_effects=True, vmem_limit_bytes=VMEM_BYTES
        ),
        name="unet",
    )(*args)
    if full:
        result = pl.pallas_call(
            write_out,
            out_shape=shapes,
            in_specs=[hbm] * 4,
            out_specs=(hbm,) * 4,
            scratch_shapes=[*[pltpu.VMEM(r.shape, r.dtype) for r in shapes], dma((8,))],
            compiler_params=pltpu.CompilerParams(vmem_limit_bytes=VMEM_BYTES),
            name="write_out",
        )(*result)
    pred, grad_fine, grad_coarse, grad_head = result
    result = (pred, grad_fine.T, grad_coarse, grad_head.T)
    if not full:
        pred, grad_fine, grad_coarse, grad_head = result
        grads = lax.psum((grad_fine, grad_coarse, grad_head), ("patch", "sub", "rep"))
        result = (pred, *grads)
    return tuple(result)


def solution(mesh):
    pixel = P(None, ("patch", "sub"))
    maps = P(("parts", "rep"), None, ("patch", "sub"))
    ring = (mesh.shape["patch"], mesh.shape["sub"])
    return jax.shard_map(
        partial(on_device, ring, mesh.shape["rep"]),
        mesh=mesh,
        in_specs=(maps, pixel, pixel, pixel, pixel, P(), P(), P(), maps),
        out_specs=(maps, P("parts", None), P("parts", None), P("parts", None)),
        check_vma=False,
    )
```
